512 devices in a mesh: section: 2 (over core), context: 32 (over z, y_lo), tensor: 8 (over x, y_hi).
Axes of the slice: x: 4, y: 4 (y_hi: 2, y_lo: 2; y = y_hi * 2 + y_lo), z: 16, core: 2. Of those that a mesh axis runs over, the one named last changes fastest.
Arguments:
- queries: bfloat16 [2, 512, 8192], P('section', 'context', 'tensor'), may hold values from -6 to 6
- turn_keys: bfloat16 [2, 512, 1024], P('section', 'context', 'tensor'), may hold values from -12 to 12
- turn_values: bfloat16 [2, 512, 1024], P('section', 'context', 'tensor'), may hold values from -6 to 6
- cache_keys: bfloat16 [2, 65536, 1024], P('section', 'context', 'tensor'), may hold values from -6 to 6
- cache_values: bfloat16 [2, 65536, 1024], P('section', 'context', 'tensor'), may hold values from -6 to 6
- positions: int32 [2, 512], P('section'), may hold values from 0 to 511, each once within a row
- span_bounds: int32 [2, 4, 2], P('section'), may hold values from 0 to 512, as said below
- residual: bfloat16 [2, 512, 8192], P('section', 'tensor', 'context'), may hold values from -3 to 3
- out_weight: bfloat16 [2, 8192, 8192], P('section', 'tensor', 'context'), may hold values from -0.0625 to 0.0625
Outputs:
- handed: bfloat16 [2, 512, 8192], P('section', 'tensor', 'context')
The draws below stay inside these ranges and needn't reach their ends.
Inputs may be any that keep to these rules, and one draw needn't show every extreme that they name: `positions`: each row lists every position of the turn once. `span_bounds`: span j lies within positions j * 128 to (j + 1) * 128, is at least 32 positions long; the first span starts at 0 and the last ends at 512.
All inputs are finite; a program needn't handle non-finite values.
Results may differ from the reference program's by a relative error of at most 0.0035.
Values may be sent and summed in bfloat16 or wider, within the bound.
A program may use at most 64 MiB of HBM per device.

```python
import jax
import jax.numpy as jnp
from jax import lax

D = 8192
HEADS = 64
KV_HEADS = 8
HD = 128
CACHE_DEV = 2048
SPANS = 4
TURN = 512
CACHE = 65536
N_SECTION = 2
N_CONTEXT = 32


def draw_queries(key, part):
    key = jax.random.fold_in(key, 1)
    shape = (N_SECTION, TURN, HEADS, HD)
    values = jnp.clip(1.7 * jax.random.normal(key, shape, jnp.float32), -6.0, 6.0)
    return values.reshape(N_SECTION, TURN, HEADS * HD).astype(jnp.bfloat16)


def draw_cache_keys(key, part):
    key = jax.random.fold_in(key, 2)
    shape = (N_SECTION, CACHE, KV_HEADS, HD)
    values = jnp.clip(1.35 * jax.random.normal(key, shape, jnp.float32), -6.0, 6.0)
    return values.reshape(N_SECTION, CACHE, KV_HEADS * HD).astype(jnp.bfloat16)


def draw_span_bounds(key, part):
    key = jax.random.fold_in(key, 3)
    slot = TURN // SPANS
    split_keys = jax.random.split(key, 2)
    lengths = jax.random.randint(split_keys[0], (N_SECTION, SPANS), slot // 4, slot)
    room = slot - lengths
    offsets = jax.random.randint(split_keys[1], (N_SECTION, SPANS), 0, 1 << 20) % (room + 1)
    number = jnp.arange(SPANS)[None, :]
    offsets = jnp.where(number == 0, 0, jnp.where(number == SPANS - 1, room, offsets))
    starts = number * slot + offsets
    return jnp.stack([starts, starts + lengths], axis=-1).astype(jnp.int32)


def level_of(key, shape, cuts, low, top_value):
    factor_of = 1.0
    for dim, shards_of in cuts:
        steps = jax.random.uniform(jax.random.fold_in(jax.random.fold_in(key, 6), dim), (shards_of,), jnp.float32, low / len(cuts), top_value / len(cuts))
        factor_of = factor_of * jnp.repeat(jnp.exp(steps), shape[dim] // shards_of).reshape((-1,) + (1,) * (len(shape) - 1 - dim))
    return factor_of


def gaussian(own_key, shape, width, most, cuts=(), dtype=jnp.bfloat16):
    loudness = level_of(own_key, shape, cuts, -0.22, 0.18) if cuts else 1.0
    values = jax.random.normal(own_key, shape, jnp.float32) * width * loudness
    return jnp.minimum(jnp.maximum(values, -most), most).astype(dtype)


def setup_inputs(seed: int = 0) -> dict:
    seeds = jax.random.split(jax.random.key(seed), 10)
    queries = draw_queries(jax.random.fold_in(seeds[9], 71), 0)
    turn_keys = gaussian(seeds[1], (N_SECTION, TURN, KV_HEADS * HD), 2.0, 12.0, ((0, 2), (1, 32), (2, 8)))
    turn_values = gaussian(seeds[2], (N_SECTION, TURN, KV_HEADS * HD), 1.0, 6.0, ((0, 2), (1, 32), (2, 8)))
    cache_keys = draw_cache_keys(jax.random.fold_in(seeds[9], 71), 0)
    cache_values = gaussian(seeds[4], (N_SECTION, CACHE, KV_HEADS * HD), 1.0, 6.0, ((0, 2), (1, 32), (2, 8)))
    positions = jax.vmap(lambda own: jax.random.permutation(own, TURN))(jax.random.split(seeds[5], N_SECTION)).reshape((N_SECTION, TURN)).astype(jnp.int32)
    span_bounds = draw_span_bounds(jax.random.fold_in(seeds[9], 71), 0)
    residual = gaussian(seeds[7], (N_SECTION, TURN, D), 0.5, 3.0, ((0, 2), (1, 8), (2, 32)))
    out_weight = gaussian(seeds[8], (N_SECTION, HEADS * HD, D), (HEADS * HD) ** -0.5, 0.0625, ((0, 2), (1, 8), (2, 32)))
    return dict(queries=queries, turn_keys=turn_keys, turn_values=turn_values, cache_keys=cache_keys, cache_values=cache_values, positions=positions, span_bounds=span_bounds, residual=residual, out_weight=out_weight)


NEG = -1e30


def visibility(position, bounds):
    starts = bounds[:, 0]
    ends = bounds[:, 1]
    inside = ((starts[None, :] <= position[:, None]) & (position[:, None] < ends[None, :])).astype(jnp.float32)
    same = jnp.dot(inside, inside.T, preferred_element_type=jnp.float32) > 0.5
    return (position[None, :] <= position[:, None]) | same


def attend(query, keys, values, allowed):
    scores = jnp.einsum('rqd,kd->rqk', query.astype(jnp.float32), keys.astype(jnp.float32)) * (HD ** -0.5)
    if allowed is not None:
        scores = jnp.where(allowed[:, None, :], scores, NEG)
    top = jnp.max(scores, axis=-1)
    expo = jnp.exp(scores - top[..., None])
    total = jnp.sum(expo, axis=-1)
    probs = expo.astype(jnp.bfloat16)
    weighted = jnp.einsum('rqk,kd->rqd', probs.astype(jnp.float32), values.astype(jnp.float32))
    return weighted / total[..., None], top + jnp.log(total)


def merge(first, second):
    joined = jnp.logaddexp(first[1], second[1])
    result = first[0] * jnp.exp(first[1] - joined)[..., None] + second[0] * jnp.exp(second[1] - joined)[..., None]
    return result, joined


def one_section(queries, turn_keys, turn_values, cache_keys, cache_values, positions, span_bounds, residual, out_weight):
    group = HEADS // KV_HEADS
    query_heads = queries.reshape(TURN, KV_HEADS, group, HD).transpose(1, 0, 2, 3)
    turn_key_heads = turn_keys.reshape(TURN, KV_HEADS, HD).transpose(1, 0, 2)
    turn_value_heads = turn_values.reshape(TURN, KV_HEADS, HD).transpose(1, 0, 2)
    cache_key_heads = cache_keys.reshape(N_CONTEXT, CACHE_DEV, KV_HEADS, HD).transpose(2, 0, 1, 3)
    cache_value_heads = cache_values.reshape(N_CONTEXT, CACHE_DEV, KV_HEADS, HD).transpose(2, 0, 1, 3)
    allowed = visibility(positions, span_bounds)

    def per_head(items):
        query, key_turn, value_turn, key_cache, value_cache = items

        def absorb(state, block):
            return merge(state, attend(query, block[0], block[1], None)), 0

        start = (jnp.zeros((TURN, group, HD), jnp.float32), jnp.full((TURN, group), NEG, jnp.float32))
        state = lax.scan(absorb, start, (key_cache, value_cache))[0]
        return merge(state, attend(query, key_turn, value_turn, allowed))[0]

    results = lax.map(per_head, (query_heads, turn_key_heads, turn_value_heads, cache_key_heads, cache_value_heads))
    attended = results.transpose(1, 0, 2, 3).reshape(TURN, HEADS * HD).astype(jnp.bfloat16)
    projected = jnp.dot(attended, out_weight, preferred_element_type=jnp.float32)
    return (residual.astype(jnp.float32) + projected).astype(jnp.bfloat16)


def reference(queries, turn_keys, turn_values, cache_keys, cache_values, positions, span_bounds, residual, out_weight):
    layers = [one_section(queries[section], turn_keys[section], turn_values[section], cache_keys[section], cache_values[section], positions[section], span_bounds[section], residual[section], out_weight[section]) for section in range(N_SECTION)]
    return jnp.stack([layers[(section - 1) % N_SECTION] for section in range(N_SECTION)])
```

```python
import functools
import math

import jax
import jax.numpy as jnp
from jax import lax
from jax.experimental import pallas as pl
from jax.experimental.pallas import tpu as pltpu
from jax.sharding import PartitionSpec as P

MESH = pl.DeviceIdType.MESH
HD = 128
NEG = -1e30
NZ = 16
KEYS = 2048
ROWS = 16
TILE = 256
BLOCK = 512
PACK = HD + 16
SCALE = math.log2(math.e) / math.sqrt(HD)
NT = (((1,), (1,)), ((), ()))
F32, BF16 = jnp.float32, jnp.bfloat16

ORDER = [
    ("A", 0), ("B", 0), ("A", 1), ("A", -1), ("A", 2), ("A", -2), ("B", 1), ("B", -1),
    ("A", 5), ("A", -5), ("A", 3), ("A", -3), ("B", 2), ("B", -2), ("A", 4), ("A", -4),
    ("B", 5), ("B", -5), ("A", 6), ("A", -6), ("A", 7), ("A", -7), ("A", 8), ("B", 3),
    ("B", -3), ("B", 4), ("B", -4), ("B", 8), ("B", 6), ("B", -6), ("B", 7), ("B", -7),
]
SLOT = {chunk: i for i, chunk in enumerate(ORDER)}
TILES = len(ORDER) // 2
XORDER = [0, 1, -1, 2, -2, 5, -5, 3, -3, 4, -4, 6, -6, 7, -7, 8]
XSLOT = {o: i for i, o in enumerate(XORDER)}
HOP = {8: 3, 7: 2, 6: 1, 5: 5, 4: 2, 3: 1, 2: 2, 1: 1}


def pack(values, total, offset):
    row = lax.broadcasted_iota(jnp.int32, (16, values.shape[1]), 0)
    total_hi = total.astype(BF16).astype(F32)
    offset_hi = offset.astype(BF16).astype(F32)
    tail = jnp.where(row == 0, total_hi, 0.0)
    tail = jnp.where(row == 1, total - total_hi, tail)
    tail = jnp.where(row == 2, offset_hi, tail)
    tail = jnp.where(row == 3, offset - offset_hi, tail)
    return values.astype(BF16), tail.astype(BF16)


def merge(blocks):
    tails = [b[HD:PACK].astype(F32) for b in blocks]
    totals = [t[0:1] + t[1:2] for t in tails]
    offsets = [t[2:3] + t[3:4] for t in tails]
    top = functools.reduce(jnp.maximum, offsets)
    factors = [jnp.exp2(o - top) for o in offsets]
    total = sum(t * f for t, f in zip(totals, factors))
    values = sum(b[:HD].astype(F32) * f for b, f in zip(blocks, factors))
    return values, total, top


def kernel(
    q_ref, tk_ref, tv_ref, k_hbm, v_hbm, pos_ref, span_ref, res_hbm, w_hbm,
    out_ref,
    qbuf, kk, vraw, vt, s0, s1, m0, m1, limit, limit_rows, key_pos, obuf, arecv, rrecv, xbuf, wbuf, proj, pbuf, res, rbuf,
    load_sem, q_recv, a_recv, r_recv, x_recv, w_recv, p_recv, res_recv, send,
):
    s = lax.axis_index("section")
    c = lax.axis_index("context")
    t = lax.axis_index("tensor")
    z, y = c // 2, lax.rem(c, 2)

    def along(distance):
        return (s, lax.rem(z + distance + 2 * NZ, NZ) * 2 + y, t)

    partner = (s, z * 2 + 1 - y, t)

    def plane(to_y, to_t):
        return (1 - s, z * 2 + to_y, to_t)

    def remote(src, dst, send_sem, recv_sem, device):
        return pltpu.make_async_remote_copy(src, dst, send_sem, recv_sem, device_id=device, device_id_type=MESH)

    barrier = pltpu.get_barrier_semaphore()
    for d in (5, 2, 1, 3):
        for sign in (1, -1):
            pl.semaphore_signal(barrier, inc=1, device_id=along(sign * d), device_id_type=MESH)
    pl.semaphore_signal(barrier, inc=1, device_id=partner, device_id_type=MESH)
    for to_y in range(2):
        for to_t in range(8):
            pl.semaphore_signal(barrier, inc=1, device_id=plane(to_y, to_t), device_id_type=MESH)

    loads = [
        pltpu.make_async_copy(v_hbm, vraw, load_sem.at[0]),
        pltpu.make_async_copy(k_hbm, kk.at[pl.ds(0, KEYS), pl.ds(0, HD)], load_sem.at[1]),
        pltpu.make_async_copy(k_hbm, kk.at[pl.ds(0, KEYS), pl.ds(HD, HD)], load_sem.at[2]),
        pltpu.make_async_copy(w_hbm, wbuf.at[y], load_sem.at[3]),
        pltpu.make_async_copy(res_hbm, res, load_sem.at[4]),
    ]
    for load in loads:
        load.start()
    for h in range(8):
        qbuf[0, pl.ds(h * ROWS, ROWS), :] = q_ref[:, h * HD : (h + 1) * HD]

    pl.semaphore_wait(barrier, 25)

    def q_send(src, dst, device, which):
        remote(qbuf.at[src], qbuf.at[dst], send.at[which], q_recv.at[dst], device).start()

    def q_wait(slot):
        remote(qbuf.at[slot], qbuf.at[slot], send.at[0], q_recv.at[slot], partner).wait_recv()

    for d in (5, 2, 1):
        for sign in (1, -1):
            q_send(0, SLOT["A", -sign * d], along(sign * d), 0)
        if d == 5:
            q_send(0, SLOT["B", 0], partner, 1)

    def arrive(d):
        for sign in (1, -1):
            src = SLOT["A", -sign * d]
            q_wait(src)
            for far, step in {5: ((7, 2), (6, 1)), 2: ((4, 2), (3, 1))}.get(d, ()):
                q_send(src, SLOT["A", -sign * far], along(sign * step), 0)
        if d == 5:
            q_send(SLOT["A", 5] + 1 - s, SLOT["A", 8], along((1 - 2 * s) * 3), 0)
        for sign in (1, -1):
            q_send(SLOT["A", -sign * d], SLOT["B", -sign * d], partner, 1)

    def arrive_last():
        q_wait(SLOT["A", 8])
        q_send(SLOT["A", 8], SLOT["B", 8], partner, 1)

    row = lax.broadcasted_iota(jnp.int32, (16, KEYS + ROWS), 0)
    vt[HD:PACK, :] = jnp.where(row == 0, 1.0, 0.0).astype(BF16)
    vt[0:HD, KEYS : KEYS + ROWS] = tv_ref[...].astype(F32).T.astype(BF16)
    kk[KEYS : KEYS + ROWS, 0:HD] = tk_ref[...]
    kk[KEYS : KEYS + ROWS, HD : 2 * HD] = tk_ref[...]
    position = pos_ref[...].astype(F32)
    seen = position + 1.0
    for j in range(4):
        start = span_ref[j, 0].astype(F32)
        end = span_ref[j, 1].astype(F32)
        inside = (start <= position) & (position < end)
        seen = jnp.where(inside, jnp.maximum(seen, end), seen)
    lane = lax.broadcasted_iota(jnp.int32, (32, 512), 1)
    chunk_row = lax.broadcasted_iota(jnp.int32, (32, 512), 0)
    spread = jnp.where(lane // ROWS == chunk_row, seen, 0.0)
    spread_hi = spread.astype(BF16)
    spread_lo = (spread - spread_hi.astype(F32)).astype(BF16)
    pick = jnp.where(
        lax.rem(lax.broadcasted_iota(jnp.int32, (512, HD), 0), ROWS)
        == lax.rem(lax.broadcasted_iota(jnp.int32, (512, HD), 1), ROWS),
        1.0,
        0.0,
    ).astype(BF16)
    limit_rows[...] = jnp.dot(spread_hi, pick, preferred_element_type=F32) + jnp.dot(
        spread_lo, pick, preferred_element_type=F32
    )
    key_lane = lax.broadcasted_iota(jnp.int32, (ROWS, 512), 1)
    key_row = lax.broadcasted_iota(jnp.int32, (ROWS, 512), 0)
    own = jnp.where(key_lane == key_row + c * ROWS, position, 0.0)
    key_pos[...] = jnp.broadcast_to(jnp.sum(own, axis=1, keepdims=True), (ROWS, HD))
    for i, (kind, o) in enumerate(ORDER):
        chunk = lax.rem(z + o + NZ, NZ) * 2 + (y if kind == "A" else 1 - y)
        limit[i // 2, :, (i % 2) * HD : (i % 2 + 1) * HD] = jnp.broadcast_to(
            limit_rows[pl.ds(chunk, 1), :], (8, HD)
        )
    loads[0].wait()
    for b in range(KEYS // HD):
        vt[0:HD, b * HD : (b + 1) * HD] = vraw[b * HD : (b + 1) * HD, :].T
    loads[1].wait()
    loads[2].wait()

    def step(scores_of, s_new, m_new, values_of, s_old, m_old):
        top = acc = offset = query = None
        if scores_of is not None:
            scaled = qbuf[pl.ds(2 * scores_of, 2)].reshape(TILE, HD).astype(F32) * SCALE
            high = scaled.astype(BF16)
            query = jnp.concatenate([high, (scaled - high.astype(F32)).astype(BF16)], axis=1)
        if values_of is not None:
            offset = jnp.ceil(jnp.max(m_old[...], axis=0, keepdims=True))
        for first in range(0, KEYS + ROWS, BLOCK):
            keys = min(BLOCK, KEYS + ROWS - first)
            if scores_of is not None:
                scores = lax.dot_general(kk[first : first + keys, :], query, NT, preferred_element_type=F32)
                if first == KEYS:
                    far = jnp.concatenate([key_pos[...], key_pos[...]], axis=1)
                    scores = jnp.where(far < limit[scores_of][0:1], scores, NEG)
                s_new[first : first + keys, :] = scores
                most = jnp.max(scores.reshape(keys // 8, 8, TILE), axis=0)
                top = most if top is None else jnp.maximum(top, most)
            if values_of is not None:
                probs = jnp.exp2(s_old[first : first + keys, :] - offset).astype(BF16)
                part = jnp.dot(vt[:, first : first + keys], probs, preferred_element_type=F32)
                acc = part if acc is None else acc + part
        if scores_of is not None:
            m_new[...] = top
        if values_of is not None:
            values, tail = pack(acc[:HD], acc[HD : HD + 1], offset)
            for half in range(2):
                obuf[2 * values_of + half, 0:HD, :] = values[:, half * HD : (half + 1) * HD]
                obuf[2 * values_of + half, HD:PACK, :] = tail[:, half * HD : (half + 1) * HD]

    before = {i: [] for i in range(TILES)}
    after = {i: [] for i in range(TILES)}
    before[0].append(lambda: q_wait(SLOT["B", 0]))
    before[1].append(lambda: arrive(1))
    before[2].append(lambda: arrive(2))
    before[3].append(lambda: arrive(5))
    before[5].append(lambda: arrive(3))
    before[6].append(lambda: arrive(4))
    before[8].append(lambda: arrive(6))
    before[9].append(lambda: arrive(7))
    before[10].append(arrive_last)
    for i, (kind, o) in enumerate(ORDER):
        if kind == "B" and o != 0:
            before[i // 2].append(functools.partial(q_wait, i))
        if kind == "A":
            after[i // 2].append(
                functools.partial(
                    lambda src, dst: remote(obuf.at[src], arecv.at[dst], send.at[2], a_recv.at[dst], partner).start(),
                    i,
                    XSLOT[o],
                )
            )

    def run(events, tile, j=None, of=None):
        if j is None:
            for event in events[tile]:
                event()
            return
        for at in range(TILES // 2 - 1):
            todo = events[2 * at + of]
            if todo:

                @pl.when(j == at)
                def _(todo=todo):
                    for event in todo:
                        event()

    run(before, 0)
    step(0, s0, m0, None, None, None)

    def two(j, carry):
        run(before, None, j, 1)
        step(2 * j + 1, s1, m1, 2 * j, s0, m0)
        run(after, None, j, 0)
        run(before, None, j, 2)
        step(2 * j + 2, s0, m0, 2 * j + 1, s1, m1)
        run(after, None, j, 1)
        return carry

    lax.fori_loop(0, TILES // 2 - 1, two, 0)
    run(before, TILES - 1)
    step(TILES - 1, s1, m1, TILES - 2, s0, m0)
    run(after, TILES - 2)
    step(None, None, None, TILES - 1, s1, m1)
    run(after, TILES - 1)

    loads[3].wait()
    remote(wbuf.at[y], wbuf.at[y], send.at[3], w_recv, partner).start()
    loads[4].wait()
    remote(res, rbuf, send.at[4], res_recv, plane(y, t)).start()

    def a_wait(slot):
        remote(obuf.at[0], arecv.at[slot], send.at[2], a_recv.at[slot], partner).wait_recv()

    def r_wait(side, d):
        remote(obuf.at[0], rrecv.at[side, d], send.at[5], r_recv.at[side, d], partner).wait_recv()

    def reduce_to(side, d, slot, aslot, parts):
        a_wait(aslot)
        for part in parts:
            r_wait(side, part)
        values, total, offset = merge([obuf[slot], arecv[aslot]] + [rrecv[side, part] for part in parts])
        values, tail = pack(values, total, offset)
        obuf[slot, 0:HD, :] = values
        obuf[slot, HD:PACK, :] = tail
        device = along((1 - 2 * side) * HOP[d])
        remote(obuf.at[slot], rrecv.at[side, d], send.at[5], r_recv.at[side, d], device).start()

    def signed(side, d):
        return d * (1 - 2 * side)

    reduce_to(s, 8, SLOT["B", 8], XSLOT[8], [])
    for d in (7, 6, 4, 3):
        for side in range(2):
            reduce_to(side, d, SLOT["B", signed(side, d)], XSLOT[signed(side, d)], [])
    for side in range(2):
        reduce_to(side, 1, SLOT["B", signed(side, 1)], XSLOT[signed(side, 1)], [])
    reduce_to(1 - s, 5, SLOT["B", 5] + 1 - s, XSLOT[5] + 1 - s, [7, 6])
    reduce_to(s, 5, SLOT["B", 5] + s, XSLOT[5] + s, [7, 6, 8])
    for side in range(2):
        reduce_to(side, 2, SLOT["B", signed(side, 2)], XSLOT[signed(side, 2)], [4, 3])
    a_wait(0)
    for d in (1, 2, 5):
        for side in range(2):
            r_wait(side, d)
    values, total, _ = merge(
        [obuf[SLOT["B", 0]], arecv[0]] + [rrecv[side, d] for d in (1, 2, 5) for side in range(2)]
    )
    xbuf[0] = (values / total).T.astype(BF16)

    def x_send(src, dst, device):
        remote(xbuf.at[src], xbuf.at[dst], send.at[6], x_recv.at[dst], device).start()

    def x_wait(slot):
        remote(xbuf.at[slot], xbuf.at[slot], send.at[6], x_recv.at[slot], partner).wait_recv()

    for d in (5, 2, 1):
        for sign in (1, -1):
            x_send(0, XSLOT[-sign * d], along(sign * d))

    def x_arrive(d):
        for sign in (1, -1):
            src = XSLOT[-sign * d]
            x_wait(src)
            for far, step_ in {5: ((7, 2), (6, 1)), 2: ((4, 2), (3, 1))}.get(d, ()):
                x_send(src, XSLOT[-sign * far], along(sign * step_))
        if d == 5:
            x_send(XSLOT[5] + 1 - s, XSLOT[8], along((1 - 2 * s) * 3))

    def project(offsets):
        rows = jnp.concatenate(
            [jnp.concatenate([xbuf[XSLOT[o], h * ROWS : (h + 1) * ROWS, :] for h in range(8)], axis=1) for o in offsets],
            axis=0,
        )
        first = XSLOT[offsets[0]] * ROWS
        for to_y in range(2):
            done = jnp.dot(rows, wbuf[to_y], preferred_element_type=F32)
            proj[to_y, first : first + ROWS * len(offsets), :] = done.astype(BF16)
        for i, o in enumerate(offsets):
            chip = lax.rem(z + o + NZ, NZ)
            place = (lax.rem(chip, 2) * 2 + 1 - y) * ROWS
            for to_y in range(2):
                remote(
                    proj.at[to_y, pl.ds(first + i * ROWS, ROWS)],
                    pbuf.at[t, pl.ds(pl.multiple_of(place, ROWS), ROWS)],
                    send.at[7],
                    p_recv,
                    plane(to_y, chip // 2),
                ).start()

    x_arrive(1)
    x_arrive(2)
    remote(wbuf.at[y], wbuf.at[1 - y], send.at[3], w_recv, partner).wait_recv()
    project([0, 1, -1, 2, -2])
    x_arrive(5)
    project([5, -5])
    x_arrive(3)
    project([3, -3])
    x_arrive(4)
    project([4, -4])
    x_arrive(6)
    project([6, -6])
    x_arrive(7)
    project([7, -7])
    x_wait(XSLOT[8])
    project([8])

    remote(res, rbuf, send.at[4], res_recv, partner).wait_recv()
    pltpu.make_async_copy(pbuf, pbuf, p_recv).wait()
    total = rbuf[...].astype(F32)
    for group in range(8):
        total = total + pbuf[group].astype(F32)
    out_ref[...] = total.astype(BF16)

    for which, ref in (
        (0, qbuf.at[pl.ds(0, 15)]), (1, qbuf.at[pl.ds(0, 16)]), (2, obuf.at[pl.ds(0, 16)]), (3, wbuf.at[0]),
        (4, res), (5, obuf.at[pl.ds(0, 15)]), (6, xbuf.at[pl.ds(0, 15)]), (7, proj),
    ):
        pltpu.make_async_copy(ref, ref, send.at[which]).wait()


def local(queries, turn_keys, turn_values, cache_keys, cache_values, positions, span_bounds, residual, out_weight):
    vmem = pl.BlockSpec(memory_space=pltpu.VMEM)
    smem = pl.BlockSpec(memory_space=pltpu.SMEM)
    hbm = pl.BlockSpec(memory_space=pl.ANY)
    dma = pltpu.SemaphoreType.DMA
    out = pl.pallas_call(
        kernel,
        name="prefill",
        out_shape=jax.ShapeDtypeStruct((64, 256), BF16),
        in_specs=[vmem, vmem, vmem, hbm, hbm, vmem, smem, hbm, hbm],
        out_specs=vmem,
        scratch_shapes=[
            pltpu.VMEM((32, HD, HD), BF16),
            pltpu.VMEM((KEYS + ROWS, 2 * HD), BF16),
            pltpu.VMEM((KEYS, HD), BF16),
            pltpu.VMEM((PACK, KEYS + ROWS), BF16),
            pltpu.VMEM((KEYS + ROWS, TILE), F32),
            pltpu.VMEM((KEYS + ROWS, TILE), F32),
            pltpu.VMEM((8, TILE), F32),
            pltpu.VMEM((8, TILE), F32),
            pltpu.VMEM((TILES, 8, TILE), F32),
            pltpu.VMEM((32, HD), F32),
            pltpu.VMEM((ROWS, HD), F32),
            pltpu.VMEM((32, PACK, HD), BF16),
            pltpu.VMEM((16, PACK, HD), BF16),
            pltpu.VMEM((2, 9, PACK, HD), BF16),
            pltpu.VMEM((16, HD, HD), BF16),
            pltpu.VMEM((2, 1024, 256), BF16),
            pltpu.VMEM((2, 256, 256), BF16),
            pltpu.VMEM((8, 64, 256), BF16),
            pltpu.VMEM((64, 256), BF16),
            pltpu.VMEM((64, 256), BF16),
            dma((5,)),
            dma((32,)),
            dma((16,)),
            dma((2, 9)),
            dma((16,)),
            dma,
            dma,
            dma,
            dma((8,)),
        ],
        compiler_params=pltpu.CompilerParams(collective_id=0, has_side_effects=True, vmem_limit_bytes=48 << 20),
        cost_estimate=pl.CostEstimate(flops=9 * 10**9, bytes_accessed=2 << 20, transcendentals=8 << 20),
    )(
        queries[0], turn_keys[0], turn_values[0], cache_keys[0], cache_values[0], positions, span_bounds[0], residual[0],
        out_weight[0],
    )
    return out[None]


def solution(mesh):
    placed = (
        P("section", "context", "tensor"),
        P("section", "context", "tensor"),
        P("section", "context", "tensor"),
        P("section", "context", "tensor"),
        P("section", "context", "tensor"),
        P("section", None),
        P("section", None, None),
        P("section", "tensor", "context"),
        P("section", "tensor", "context"),
    )
    return jax.shard_map(
        local,
        mesh=mesh,
        in_specs=placed,
        out_specs=P("section", "tensor", "context"),
        check_vma=False,
    )
```

```python
import functools
import math

import jax
import jax.numpy as jnp
from jax import lax
from jax.experimental import pallas as pl
from jax.experimental.pallas import tpu as pltpu
from jax.sharding import PartitionSpec as P

MESH = pl.DeviceIdType.MESH
HD = 128
NEG = -1e30
NZ = 16
KEYS = 2048
ROWS = 16
TILE = 256
BLOCK = 512
PACK = HD + 16
SCALE = math.log2(math.e) / math.sqrt(HD)
NT = (((1,), (1,)), ((), ()))
F32, BF16 = jnp.float32, jnp.bfloat16

ORDER = [
    ("A", 0), ("B", 0), ("A", 1), ("A", -1), ("A", 2), ("A", -2), ("A", 5), ("A", -5),
    ("B", 1), ("B", -1), ("A", 3), ("A", -3), ("A", 4), ("A", -4), ("B", 2), ("B", -2),
    ("A", 6), ("A", -6), ("A", 7), ("A", -7), ("A", 8), ("B", 3), ("B", -3), ("B", 4),
    ("B", -4), ("B", 5), ("B", -5), ("B", 6), ("B", -6), ("B", 7), ("B", -7), ("B", 8),
]
SLOT = {chunk: i for i, chunk in enumerate(ORDER)}
TILES = len(ORDER) // 2
XORDER = [0, 1, -1, 2, -2, 5, -5, 3, -3, 4, -4, 6, -6, 7, -7, 8]
XSLOT = {o: i for i, o in enumerate(XORDER)}
FORWARD = {5: ((7, 2), (6, 1)), 2: ((4, 2), (3, 1))}
HOP = {8: 3, 7: 2, 6: 1, 5: 5, 4: 2, 3: 1, 2: 2, 1: 1}


def pack(values, total, offset):
    row = lax.broadcasted_iota(jnp.int32, (16, values.shape[1]), 0)
    total_hi = total.astype(BF16).astype(F32)
    offset_hi = offset.astype(BF16).astype(F32)
    tail = jnp.where(row == 0, total_hi, 0.0)
    tail = jnp.where(row == 1, total - total_hi, tail)
    tail = jnp.where(row == 2, offset_hi, tail)
    tail = jnp.where(row == 3, offset - offset_hi, tail)
    return values.astype(BF16), tail.astype(BF16)


def merge(blocks):
    tails = [b[HD:PACK].astype(F32) for b in blocks]
    totals = [t[0:1] + t[1:2] for t in tails]
    offsets = [t[2:3] + t[3:4] for t in tails]
    top = functools.reduce(jnp.maximum, offsets)
    factors = [jnp.exp2(o - top) for o in offsets]
    total = sum(t * f for t, f in zip(totals, factors))
    values = sum(b[:HD].astype(F32) * f for b, f in zip(blocks, factors))
    return values, total, top


def kernel(
    q_hbm, tk_hbm, tv_hbm, k_hbm, v_hbm, pos_hbm, span_hbm, res_hbm, w_hbm,
    out_ref,
    q_ref, tv_ref, pos_ref, span_ref, qbuf, kk, vraw, vt, s0, s1, m0, m1, limit, limit_rows, key_pos, obuf, arecv, rrecv, xbuf, wbuf, proj, pbuf, res, rbuf,
    load_sem, q_recv, a_recv, r_recv, x_recv, w_recv, p_recv, res_recv, send,
):
    s = lax.axis_index("section")
    c = lax.axis_index("context")
    t = lax.axis_index("tensor")
    z, y = c // 2, lax.rem(c, 2)

    def along(distance):
        return (s, lax.rem(z + distance + 2 * NZ, NZ) * 2 + y, t)

    partner = (s, z * 2 + 1 - y, t)

    def plane(to_y, to_t):
        return (1 - s, z * 2 + to_y, to_t)

    def remote(src, dst, send_sem, recv_sem, device):
        return pltpu.make_async_remote_copy(src, dst, send_sem, recv_sem, device_id=device, device_id_type=MESH)

    barrier = pltpu.get_barrier_semaphore()
    for d in (5, 2, 1, 3):
        for sign in (1, -1):
            pl.semaphore_signal(barrier, inc=1, device_id=along(sign * d), device_id_type=MESH)
    pl.semaphore_signal(barrier, inc=1, device_id=partner, device_id_type=MESH)
    for to_y in range(2):
        for to_t in range(8):
            pl.semaphore_signal(barrier, inc=1, device_id=plane(to_y, to_t), device_id_type=MESH)

    loads = [
        pltpu.make_async_copy(q_hbm, q_ref, load_sem.at[5]),
        pltpu.make_async_copy(pos_hbm, pos_ref, load_sem.at[6]),
        pltpu.make_async_copy(tv_hbm, tv_ref, load_sem.at[7]),
        pltpu.make_async_copy(span_hbm, span_ref, load_sem.at[10]),
        pltpu.make_async_copy(tk_hbm, kk.at[pl.ds(KEYS, ROWS), pl.ds(0, HD)], load_sem.at[8]),
        pltpu.make_async_copy(tk_hbm, kk.at[pl.ds(KEYS, ROWS), pl.ds(HD, HD)], load_sem.at[9]),
        pltpu.make_async_copy(v_hbm, vraw, load_sem.at[0]),
        pltpu.make_async_copy(k_hbm, kk.at[pl.ds(0, KEYS), pl.ds(0, HD)], load_sem.at[1]),
        pltpu.make_async_copy(k_hbm, kk.at[pl.ds(0, KEYS), pl.ds(HD, HD)], load_sem.at[2]),
        pltpu.make_async_copy(w_hbm, wbuf.at[y], load_sem.at[3]),
        pltpu.make_async_copy(res_hbm, res, load_sem.at[4]),
    ]
    for load in loads:
        load.start()
    loads[0].wait()
    for h in range(8):
        qbuf[0, pl.ds(h * ROWS, ROWS), :] = q_ref[:, h * HD : (h + 1) * HD]

    pl.semaphore_wait(barrier, 25)

    def q_send(src, dst, device, which):
        remote(qbuf.at[src], qbuf.at[dst], send.at[which], q_recv.at[dst], device).start()

    def q_wait(slot):
        remote(qbuf.at[slot], qbuf.at[slot], send.at[0], q_recv.at[slot], partner).wait_recv()

    for d in (5, 2, 1):
        for sign in (1, -1):
            q_send(0, SLOT["A", -sign * d], along(sign * d), 0)
        if d == 5:
            q_send(0, SLOT["B", 0], partner, 1)

    def arrive(kind, d):
        for sign in (1, -1):
            src = SLOT[kind, -sign * d]
            q_wait(src)
            for far, step in FORWARD.get(d, ()):
                q_send(src, SLOT[kind, -sign * far], along(sign * step), 0)
        if kind == "A" and d == 5:
            q_send(SLOT["A", 5] + 1 - s, SLOT["A", 8], along((1 - 2 * s) * 3), 0)
        if kind == "A" and d in (2, 5):
            for sign in (1, -1):
                q_send(SLOT["A", -sign * d], SLOT["B", -sign * d], partner, 1)

    def arrive_partner():
        q_wait(SLOT["B", 0])
        for sign in (1, -1):
            q_send(SLOT["B", 0], SLOT["B", -sign], along(sign), 0)

    def arrive_last():
        q_wait(SLOT["A", 8])
        q_send(SLOT["A", 8], SLOT["B", 8], partner, 1)

    for load in loads[1:6]:
        load.wait()
    row = lax.broadcasted_iota(jnp.int32, (16, KEYS + ROWS), 0)
    vt[HD:PACK, :] = jnp.where(row == 0, 1.0, 0.0).astype(BF16)
    vt[0:HD, KEYS : KEYS + ROWS] = tv_ref[...].astype(F32).T.astype(BF16)
    position = pos_ref[...].astype(F32)
    seen = position + 1.0
    for j in range(4):
        start = span_ref[0:1, j : j + 1].astype(F32)
        end = span_ref[1:2, j : j + 1].astype(F32)
        inside = (start <= position) & (position < end)
        seen = jnp.where(inside, jnp.maximum(seen, end), seen)
    lane = lax.broadcasted_iota(jnp.int32, (32, 512), 1)
    chunk_row = lax.broadcasted_iota(jnp.int32, (32, 512), 0)
    spread = jnp.where(lane // ROWS == chunk_row, seen, 0.0)
    spread_hi = spread.astype(BF16)
    spread_lo = (spread - spread_hi.astype(F32)).astype(BF16)
    pick = jnp.where(
        lax.rem(lax.broadcasted_iota(jnp.int32, (512, HD), 0), ROWS)
        == lax.rem(lax.broadcasted_iota(jnp.int32, (512, HD), 1), ROWS),
        1.0,
        0.0,
    ).astype(BF16)
    limit_rows[...] = jnp.dot(spread_hi, pick, preferred_element_type=F32) + jnp.dot(
        spread_lo, pick, preferred_element_type=F32
    )
    key_lane = lax.broadcasted_iota(jnp.int32, (ROWS, 512), 1)
    key_row = lax.broadcasted_iota(jnp.int32, (ROWS, 512), 0)
    own = jnp.where(key_lane == key_row + c * ROWS, position, 0.0)
    key_pos[...] = jnp.broadcast_to(jnp.sum(own, axis=1, keepdims=True), (ROWS, HD))
    for i, (kind, o) in enumerate(ORDER):
        chunk = lax.rem(z + o + NZ, NZ) * 2 + (y if kind == "A" else 1 - y)
        limit[i // 2, :, (i % 2) * HD : (i % 2 + 1) * HD] = jnp.broadcast_to(
            limit_rows[pl.ds(chunk, 1), :], (8, HD)
        )
    loads[6].wait()
    for b in range(KEYS // HD):
        vt[0:HD, b * HD : (b + 1) * HD] = vraw[b * HD : (b + 1) * HD, :].T
    loads[7].wait()
    loads[8].wait()

    def step(scores_of, s_new, m_new, values_of, s_old, m_old):
        top = acc = offset = query = None
        if scores_of is not None:
            scaled = qbuf[pl.ds(2 * scores_of, 2)].reshape(TILE, HD).astype(F32) * SCALE
            high = scaled.astype(BF16)
            query = jnp.concatenate([high, (scaled - high.astype(F32)).astype(BF16)], axis=1)
        if values_of is not None:
            offset = jnp.ceil(jnp.max(m_old[...], axis=0, keepdims=True))
        for first in range(0, KEYS + ROWS, BLOCK):
            keys = min(BLOCK, KEYS + ROWS - first)
            if scores_of is not None:
                scores = lax.dot_general(kk[first : first + keys, :], query, NT, preferred_element_type=F32)
                if first == KEYS:
                    far = jnp.concatenate([key_pos[...], key_pos[...]], axis=1)
                    scores = jnp.where(far < limit[scores_of][0:1], scores, NEG)
                s_new[first : first + keys, :] = scores
                most = jnp.max(scores.reshape(keys // 8, 8, TILE), axis=0)
                top = most if top is None else jnp.maximum(top, most)
            if values_of is not None:
                probs = jnp.exp2(s_old[first : first + keys, :] - offset).astype(BF16)
                part = jnp.dot(vt[:, first : first + keys], probs, preferred_element_type=F32)
                acc = part if acc is None else acc + part
        if scores_of is not None:
            m_new[...] = top
        if values_of is not None:
            values, tail = pack(acc[:HD], acc[HD : HD + 1], offset)
            for half in range(2):
                obuf[2 * values_of + half, 0:HD, :] = values[:, half * HD : (half + 1) * HD]
                obuf[2 * values_of + half, HD:PACK, :] = tail[:, half * HD : (half + 1) * HD]

    def a_wait(slot):
        remote(obuf.at[0], arecv.at[slot], send.at[2], a_recv.at[slot], partner).wait_recv()

    def r_wait(side, d):
        remote(obuf.at[0], rrecv.at[side, d], send.at[5], r_recv.at[side, d], partner).wait_recv()

    def reduce_to(side, d, slot, aslot, parts):
        a_wait(aslot)
        for part in parts:
            r_wait(side, part)
        values, total, offset = merge([obuf[slot], arecv[aslot]] + [rrecv[side, part] for part in parts])
        values, tail = pack(values, total, offset)
        obuf[slot, 0:HD, :] = values
        obuf[slot, HD:PACK, :] = tail
        device = along((1 - 2 * side) * HOP[d])
        remote(obuf.at[slot], rrecv.at[side, d], send.at[5], r_recv.at[side, d], device).start()

    def signed(side, d):
        return d * (1 - 2 * side)

    def reduce_near(d):
        for side in range(2):
            reduce_to(side, d, SLOT["B", signed(side, d)], XSLOT[signed(side, d)], [])

    before = {i: [] for i in range(TILES)}
    after = {i: [] for i in range(TILES)}
    waited = {("A", 0)}

    def at(tile, event, *chunks):
        before[tile].append(event)
        waited.update(chunks)

    at(0, arrive_partner, ("B", 0))
    for tile, kind, d in (
        (1, "A", 1), (2, "A", 2), (3, "A", 5), (4, "B", 2), (5, "A", 3), (6, "A", 4), (7, "B", 5), (8, "A", 6), (9, "A", 7),
    ):
        at(tile, functools.partial(arrive, kind, d), (kind, d), (kind, -d))
    at(10, arrive_last, ("A", 8))
    for i, (kind, o) in enumerate(ORDER):
        if (kind, o) not in waited:
            before[i // 2].append(functools.partial(q_wait, i))
        if kind == "A":
            after[i // 2].append(
                functools.partial(
                    lambda src, dst: remote(obuf.at[src], arecv.at[dst], send.at[2], a_recv.at[dst], partner).start(),
                    i,
                    XSLOT[o],
                )
            )

    before[13].append(lambda: reduce_near(3))
    before[14].append(lambda: reduce_near(4))
    before[15].append(lambda: reduce_near(1))

    def run(events, tile, j=None, of=None):
        if j is None:
            for event in events[tile]:
                event()
            return
        for at in range(TILES // 2 - 1):
            todo = events[2 * at + of]
            if todo:

                @pl.when(j == at)
                def _(todo=todo):
                    for event in todo:
                        event()

    run(before, 0)
    step(0, s0, m0, None, None, None)

    def two(j, carry):
        run(before, None, j, 1)
        step(2 * j + 1, s1, m1, 2 * j, s0, m0)
        run(after, None, j, 0)
        run(before, None, j, 2)
        step(2 * j + 2, s0, m0, 2 * j + 1, s1, m1)
        run(after, None, j, 1)
        return carry

    lax.fori_loop(0, TILES // 2 - 1, two, 0)
    run(before, TILES - 1)
    step(TILES - 1, s1, m1, TILES - 2, s0, m0)
    run(after, TILES - 2)
    step(None, None, None, TILES - 1, s1, m1)
    run(after, TILES - 1)

    loads[9].wait()
    remote(wbuf.at[y], wbuf.at[y], send.at[3], w_recv, partner).start()
    loads[10].wait()
    remote(res, rbuf, send.at[4], res_recv, plane(y, t)).start()

    reduce_to(s, 8, SLOT["B", 8], XSLOT[8], [])
    for d in (7, 6):
        reduce_near(d)
    for side in range(2):
        reduce_to(side, 2, SLOT["B", signed(side, 2)], XSLOT[signed(side, 2)], [4, 3])
    reduce_to(1 - s, 5, SLOT["B", 5] + 1 - s, XSLOT[5] + 1 - s, [7, 6])
    reduce_to(s, 5, SLOT["B", 5] + s, XSLOT[5] + s, [7, 6, 8])
    a_wait(0)
    for d in (1, 2, 5):
        for side in range(2):
            r_wait(side, d)
    values, total, _ = merge(
        [obuf[SLOT["B", 0]], arecv[0]] + [rrecv[side, d] for d in (1, 2, 5) for side in range(2)]
    )
    xbuf[0] = (values / total).T.astype(BF16)

    def x_send(src, dst, device):
        remote(xbuf.at[src], xbuf.at[dst], send.at[6], x_recv.at[dst], device).start()

    def x_wait(slot):
        remote(xbuf.at[slot], xbuf.at[slot], send.at[6], x_recv.at[slot], partner).wait_recv()

    for d in (5, 2, 1):
        for sign in (1, -1):
            x_send(0, XSLOT[-sign * d], along(sign * d))

    def x_arrive(d):
        for sign in (1, -1):
            src = XSLOT[-sign * d]
            x_wait(src)
            for far, step_ in FORWARD.get(d, ()):
                x_send(src, XSLOT[-sign * far], along(sign * step_))
        if d == 5:
            x_send(XSLOT[5] + 1 - s, XSLOT[8], along((1 - 2 * s) * 3))

    def project(offsets):
        rows = jnp.concatenate(
            [jnp.concatenate([xbuf[XSLOT[o], h * ROWS : (h + 1) * ROWS, :] for h in range(8)], axis=1) for o in offsets],
            axis=0,
        )
        first = XSLOT[offsets[0]] * ROWS
        for to_y in range(2):
            done = jnp.dot(rows, wbuf[to_y], preferred_element_type=F32)
            proj[to_y, first : first + ROWS * len(offsets), :] = done.astype(BF16)
        for i, o in enumerate(offsets):
            chip = lax.rem(z + o + NZ, NZ)
            place = (lax.rem(chip, 2) * 2 + 1 - y) * ROWS
            for to_y in range(2):
                remote(
                    proj.at[to_y, pl.ds(first + i * ROWS, ROWS)],
                    pbuf.at[t, pl.ds(pl.multiple_of(place, ROWS), ROWS)],
                    send.at[7],
                    p_recv,
                    plane(to_y, chip // 2),
                ).start()

    x_arrive(1)
    x_arrive(2)
    remote(wbuf.at[y], wbuf.at[1 - y], send.at[3], w_recv, partner).wait_recv()
    project([0, 1, -1, 2, -2])
    x_arrive(5)
    project([5, -5])
    x_arrive(3)
    project([3, -3])
    x_arrive(4)
    project([4, -4])
    x_arrive(6)
    project([6, -6])
    x_arrive(7)
    project([7, -7])
    x_wait(XSLOT[8])
    project([8])

    remote(res, rbuf, send.at[4], res_recv, partner).wait_recv()
    pltpu.make_async_copy(pbuf, pbuf, p_recv).wait()
    total = rbuf[...].astype(F32)
    for group in range(8):
        total = total + pbuf[group].astype(F32)
    out_ref[...] = total.astype(BF16)

    for which, ref in (
        (0, qbuf.at[pl.ds(0, 25)]), (1, qbuf.at[pl.ds(0, 6)]), (2, obuf.at[pl.ds(0, 16)]), (3, wbuf.at[0]),
        (4, res), (5, obuf.at[pl.ds(0, 15)]), (6, xbuf.at[pl.ds(0, 15)]), (7, proj),
    ):
        pltpu.make_async_copy(ref, ref, send.at[which]).wait()


def local(queries, turn_keys, turn_values, cache_keys, cache_values, positions, span_bounds, residual, out_weight):
    vmem = pl.BlockSpec(memory_space=pltpu.VMEM)
    hbm = pl.BlockSpec(memory_space=pl.ANY)
    dma = pltpu.SemaphoreType.DMA
    out = pl.pallas_call(
        kernel,
        name="prefill",
        out_shape=jax.ShapeDtypeStruct((64, 256), BF16),
        in_specs=[hbm] * 9,
        out_specs=vmem,
        scratch_shapes=[
            pltpu.VMEM((ROWS, 8 * HD), BF16),
            pltpu.VMEM((ROWS, HD), BF16),
            pltpu.VMEM((1, 512), jnp.int32),
            pltpu.VMEM((2, 4), jnp.int32),
            pltpu.VMEM((32, HD, HD), BF16),
            pltpu.VMEM((KEYS + ROWS, 2 * HD), BF16),
            pltpu.VMEM((KEYS, HD), BF16),
            pltpu.VMEM((PACK, KEYS + ROWS), BF16),
            pltpu.VMEM((KEYS + ROWS, TILE), F32),
            pltpu.VMEM((KEYS + ROWS, TILE), F32),
            pltpu.VMEM((8, TILE), F32),
            pltpu.VMEM((8, TILE), F32),
            pltpu.VMEM((TILES, 8, TILE), F32),
            pltpu.VMEM((32, HD), F32),
            pltpu.VMEM((ROWS, HD), F32),
            pltpu.VMEM((32, PACK, HD), BF16),
            pltpu.VMEM((16, PACK, HD), BF16),
            pltpu.VMEM((2, 9, PACK, HD), BF16),
            pltpu.VMEM((16, HD, HD), BF16),
            pltpu.VMEM((2, 1024, 256), BF16),
            pltpu.VMEM((2, 256, 256), BF16),
            pltpu.VMEM((8, 64, 256), BF16),
            pltpu.VMEM((64, 256), BF16),
            pltpu.VMEM((64, 256), BF16),
            dma((11,)),
            dma((32,)),
            dma((16,)),
            dma((2, 9)),
            dma((16,)),
            dma,
            dma,
            dma,
            dma((8,)),
        ],
        compiler_params=pltpu.CompilerParams(collective_id=0, has_side_effects=True, vmem_limit_bytes=60 << 20),
        cost_estimate=pl.CostEstimate(flops=9 * 10**9, bytes_accessed=2 << 20, transcendentals=8 << 20),
    )(
        queries[0], turn_keys[0], turn_values[0], cache_keys[0], cache_values[0], positions, span_bounds[0].T, residual[0],
        out_weight[0],
    )
    return out[None]


def solution(mesh):
    placed = (
        P("section", "context", "tensor"),
        P("section", "context", "tensor"),
        P("section", "context", "tensor"),
        P("section", "context", "tensor"),
        P("section", "context", "tensor"),
        P("section", None),
        P("section", None, None),
        P("section", "tensor", "context"),
        P("section", "tensor", "context"),
    )
    return jax.shard_map(
        local,
        mesh=mesh,
        in_specs=placed,
        out_specs=P("section", "tensor", "context"),
        check_vma=False,
    )
```
